32 devices in a mesh: groups: 2 (over y), traj: 4 (over z), fsdp: 2 (over x), sub: 2 (over core).
Axes of the slice: x: 2, y: 2, z: 4, core: 2. Of those that a mesh axis runs over, the one named last changes fastest.
Arguments:
- activations: bfloat16 [4096, 8192], P(('groups', 'traj', 'fsdp', 'sub')), parts along dimension 0, may hold values from -6 to 6
- out_grads: bfloat16 [4096, 8192], P(('groups', 'traj', 'fsdp', 'sub')), parts along dimension 0, may hold values from -6 to 6
- segments: int32 [32, 128], P(('groups', 'traj', 'fsdp', 'sub')), parts along dimension 0, may hold values from 0 to 7, never falling along the last dimension, each value on 1 to 64 neighbouring positions
- loss_mask: int32 [32, 128], P(('groups', 'traj', 'fsdp', 'sub')), parts along dimension 0, may hold values 0 or 1
- proj_in: bfloat16 [64, 8192], P(None, ('fsdp', 'sub')), may hold values from -0.0625 to 0.0625
- proj_out: bfloat16 [64, 8192], P(None, ('fsdp', 'sub')), may hold values from -0.0625 to 0.0625
- queries: float32 [128, 4096], P(('groups', 'traj')), parts along dimension 0, may hold values from -0.375 to 0.375
Outputs:
- scores: float32 [128, 128], P('groups', ('traj', 'fsdp', 'sub')), parts along dimension 0
The draws below stay inside these ranges and needn't reach their ends.
There are 2 independent parts, one for each index of `groups`. The reference program is written for one: setup_inputs(seed, part) draws one part's arguments, and reference() takes and returns one part's arrays. A program takes and returns all parts, laid end to end along the dimension named above; an argument that names none is the same for every part. Nothing has to cross between parts.
Inputs may be any that keep to these rules, and one draw needn't show every extreme that they name: `segments`: within a device's row of 128 tokens segment numbers never fall; each of the 8 trajectories holds 1 to 64 tokens and one holds exactly 64.
All inputs are finite; a program needn't handle non-finite values. No bound on the sum of `loss_mask` on one device may be relied on, other than what follows from the above.
Results may differ from the reference program's by a relative error of at most 0.0003.
Values may be sent and summed in bfloat16 or wider, within the bound.
No kernel may reach another device: no remote copies, remote signals or barrier semaphores. Data moves between devices by JAX's collectives and lax.ppermute only.
A program may use at most 64 MiB of HBM per device.

```python
import math
import jax
import jax.numpy as jnp
import numpy as np
from jax import lax

D = 8192
R = 64
TOK_DEV = 128
TRAJ_DEV = 8
DEVS = 16
TOKENS = 2048
QUERIES = 64


def with_ends(array, own_key, low, high):
    longest = array.shape.index(max(array.shape))
    spots = []
    for shift in (0, 1):
        where = [jax.random.randint(jax.random.fold_in(own_key, axis), (), 0, length) for axis, length in enumerate(array.shape)]
        where[longest] = (where[longest] + shift) % array.shape[longest]
        spots.append(tuple(where))
    return array.at[spots[0]].set(low).at[spots[1]].set(high)


def block_scale(stream_key, shape, shards, smallest, largest):
    gain = 1.0
    for axis_at, shards_of in shards:
        heights = jax.random.uniform(jax.random.fold_in(jax.random.fold_in(stream_key, 6), axis_at), (shards_of,), jnp.float32, smallest / len(shards), largest / len(shards))
        gain = gain * jnp.repeat(jnp.exp(heights), shape[axis_at] // shards_of).reshape((-1,) + (1,) * (len(shape) - 1 - axis_at))
    return gain


def split_up(amount, total, reach, slope):
    weights = [(1 << 20) // math.isqrt(grade ** slope) + 1 for grade in range(2, amount + 1)]
    rest, holding = total - reach - (amount - 1), [1] * (amount - 1)
    while rest > 0:
        movable = [i for i in range(amount - 1) if holding[i] < reach]
        pool, remaining = sum([weights[i] for i in movable]), rest
        for i in movable:
            more = min(reach - holding[i], max(1, remaining * weights[i] // pool), rest)
            holding[i] = holding[i] + more
            rest = rest - more
    return np.array([reach] + holding)


def uneven_parts(stream_key, amount, total, reach, skew):
    if amount == 2:
        one = jax.random.randint(stream_key, (), max(1, total - reach), min(reach, total - 1) + 1)
        return jnp.stack([one, total - one])
    sizes = jnp.asarray(split_up(amount, total, reach, skew), jnp.int32)
    twos = (amount - 1) // 2
    donor, sink = sizes[1:1 + 2 * twos:2], sizes[2:2 + 2 * twos:2]
    slack = jnp.minimum(donor - 1, reach - sink)
    passed = jax.random.randint(jax.random.fold_in(stream_key, 1), (twos,), 0, 1 << 20) % (slack + 1)
    sizes = sizes.at[1:1 + 2 * twos:2].set(donor - passed).at[2:2 + 2 * twos:2].set(sink + passed)
    return sizes[jax.random.permutation(jax.random.fold_in(stream_key, 2), amount)]


def scatter_about(key, extent, scale, bound, cuts=(), kind=jnp.bfloat16):
    entries = jax.random.normal(key, extent, jnp.float32) * scale
    if len(cuts) > 0:
        entries = block_scale(key, extent, cuts, -0.22, 0.18) * entries
    return jnp.clip(entries, min=-bound, max=bound).astype(kind)


def setup_inputs(seed: int = 0, part: int = 0) -> dict:
    streams_of = jax.random.split(jax.random.key(seed), 8)
    part_splits = jax.random.split(jax.random.fold_in(streams_of[7], part), 8)
    return {
        "activations": scatter_about(part_splits[0], (TOKENS, D), 1.0, 6.0, ((0, 16),)),
        "out_grads": scatter_about(part_splits[1], (TOKENS, D), 1.0, 6.0, ((0, 16),)),
        "segments": jax.vmap(lambda own: jnp.searchsorted(jnp.cumsum(uneven_parts(own, TRAJ_DEV, TOK_DEV, TOK_DEV // 2, 2)), jnp.arange(TOK_DEV), side="right"))(jax.random.split(part_splits[2], DEVS)).reshape((DEVS, TOK_DEV)).astype(jnp.int32),
        "loss_mask": with_ends((jax.random.randint(part_splits[3], (DEVS, TOK_DEV), 0, 4) < 3).astype(jnp.int32), jax.random.fold_in(part_splits[3], 1), 0, 1),
        "proj_in": scatter_about(streams_of[4], (R, D), D ** -0.5, 0.0625, ((1, 4),)),
        "proj_out": scatter_about(streams_of[5], (R, D), D ** -0.5, 0.0625, ((1, 4),)),
        "queries": scatter_about(part_splits[6], (QUERIES, R * R), 0.0625, 0.375, ((0, 4),), jnp.float32),
    }


def reference(activations, out_grads, segments, loss_mask, proj_in, proj_out, queries):
    device_count = segments.shape[0]
    highest = lax.Precision.HIGHEST

    def per_device(blocks):
        act_block, grad_block, segment, mask_row = blocks
        in_coords = jnp.dot(act_block, proj_in.T, preferred_element_type=jnp.float32)
        out_coords = jnp.dot(grad_block, proj_out.T, preferred_element_type=jnp.float32)
        one_hot = (segment[:, None] == jnp.arange(TRAJ_DEV, dtype=jnp.int32)[None, :]).astype(jnp.float32)
        mask_float = mask_row.astype(jnp.float32)
        counts = jnp.dot(mask_float, one_hot, precision=highest)
        weight = mask_float * jnp.dot(one_hot, 1.0 / jnp.maximum(counts, 1.0), precision=highest)
        outer_rows = (out_coords[:, :, None] * in_coords[:, None, :]).reshape(TOK_DEV, R * R)
        return jnp.dot((one_hot * weight[:, None]).T, outer_rows, precision=highest)

    train_grads = lax.map(per_device, (activations.reshape(device_count, TOK_DEV, D), out_grads.reshape(device_count, TOK_DEV, D), segments, loss_mask))
    train_grads = train_grads.reshape(device_count * TRAJ_DEV, R * R)
    return jnp.dot(queries, train_grads.T, precision=highest)
```

```python
import jax
import jax.numpy as jnp
from jax import lax
from jax.experimental import pallas as pl
from jax.experimental.pallas import tpu as pltpu
from jax.sharding import PartitionSpec as P

TRAJ_DEV = 8
NT = (((1,), (1,)), ((), ()))
HIGHEST = lax.Precision.HIGHEST
ANY = pl.BlockSpec(memory_space=pl.ANY)
VMEM = pl.BlockSpec(memory_space=pltpu.VMEM)


def dot_nt(a, b, precision=None):
    return lax.dot_general(
        a, b, NT, precision=precision, preferred_element_type=jnp.float32
    )


def project(owners, toks, projs, base):
    rank, width = projs[0].shape
    count = toks.shape[0]

    def kernel(*refs):
        owner_ref, tok_hbm = refs[:2]
        proj_hbm = refs[2 : 2 + len(projs)]
        base_ref = refs[2 + len(projs)] if base is not None else None
        out_ref, tok, proj, tok_sem, proj_sem = refs[-5:]
        copies = []
        for i in range(len(projs)):
            columns = pl.ds(pl.multiple_of(owner_ref[i] * width, 128), width)
            pair = (
                pltpu.make_async_copy(tok_hbm.at[:, columns], tok.at[i], tok_sem.at[i]),
                pltpu.make_async_copy(proj_hbm[i], proj.at[i], proj_sem.at[i]),
            )
            for copy in pair:
                copy.start()
            copies.append(pair)
        total = None
        for i, pair in enumerate(copies):
            for copy in pair:
                copy.wait()
            part = dot_nt(proj[i], tok[i])
            total = part if total is None else total + part
        out_ref[...] = total if base is None else total + base_ref[...]

    return pl.pallas_call(
        kernel,
        out_shape=jax.ShapeDtypeStruct((rank, count), jnp.float32),
        in_specs=[pl.BlockSpec(memory_space=pltpu.SMEM), ANY]
        + [ANY] * len(projs)
        + ([VMEM] if base is not None else []),
        out_specs=VMEM,
        scratch_shapes=[
            pltpu.VMEM((len(projs), count, width), toks.dtype),
            pltpu.VMEM((len(projs), rank, width), toks.dtype),
            pltpu.SemaphoreType.DMA((len(projs),)),
            pltpu.SemaphoreType.DMA((len(projs),)),
        ],
        compiler_params=pltpu.CompilerParams(vmem_limit_bytes=32 << 20),
        cost_estimate=pl.CostEstimate(
            flops=2 * rank * count * width * len(projs),
            bytes_accessed=2 * (count + rank) * width * len(projs),
            transcendentals=0,
        ),
    )(owners, toks, *projs, *([base] if base is not None else []))


def finish(in_t, out_t, segments, loss_mask, queries):
    rank, count = in_t.shape
    asked = queries.shape[0]

    def kernel(in_ref, out_ref, seg_ref, mask_ref, q_ref, score_ref):
        own = seg_ref[...] == lax.broadcasted_iota(jnp.int32, (TRAJ_DEV, count), 0)
        masked = jnp.where(own, mask_ref[...].astype(jnp.float32), 0.0)
        counts = jnp.sum(masked, axis=1, keepdims=True)
        weight = masked * (1.0 / jnp.maximum(counts, 1.0))
        left = (out_ref[...][:, None, :] * weight[None]).reshape(rank * TRAJ_DEV, count)
        twice = jnp.concatenate([in_ref[...], in_ref[...]], axis=0)
        grads = dot_nt(left, twice, HIGHEST).reshape(rank // 2, 2, TRAJ_DEV, 2 * rank)
        low = lax.broadcasted_iota(jnp.int32, (TRAJ_DEV, 2 * rank), 1) < rank
        flat = jnp.concatenate(
            [jnp.where(low, grads[p, 0], grads[p, 1]) for p in range(rank // 2)], axis=1
        )
        score_ref[...] = dot_nt(flat, q_ref[...], HIGHEST)

    return pl.pallas_call(
        kernel,
        out_shape=jax.ShapeDtypeStruct((TRAJ_DEV, asked), jnp.float32),
        in_specs=[VMEM] * 5,
        out_specs=VMEM,
        compiler_params=pltpu.CompilerParams(vmem_limit_bytes=48 << 20),
        cost_estimate=pl.CostEstimate(
            flops=12 * TRAJ_DEV * rank * rank * (count + asked),
            bytes_accessed=4 * asked * rank * rank,
            transcendentals=0,
        ),
    )(in_t, out_t, segments, loss_mask, queries)


def gather_queries(queries, core, groups_of):
    if groups_of > 4:
        return lax.all_gather(queries, "traj", axis=0, tiled=True)
    half = queries.shape[0] // 2
    mine = lax.dynamic_slice_in_dim(queries, core * half, half, 0)
    swap = [(0, 1), (1, 0)]
    at = lax.axis_index("traj")
    out = jnp.zeros((groups_of,) + queries.shape, queries.dtype)
    out = lax.dynamic_update_slice(out, queries[None], (at, 0, 0))
    for d in range(1, groups_of):
        got = lax.ppermute(mine, "traj", [(i, (i + d) % groups_of) for i in range(groups_of)])
        other = lax.ppermute(got, "sub", swap)
        both = jnp.where(
            core == 0,
            jnp.concatenate([got, other], 0),
            jnp.concatenate([other, got], 0),
        )
        out = lax.dynamic_update_slice(
            out, both[None], ((at - d) % groups_of, 0, 0)
        )
    return out.reshape(-1, queries.shape[1])


def body(sizes, activations, out_grads, segments, loss_mask, proj_in, proj_out, queries):
    chips = sizes["fsdp"]
    x, core = lax.axis_index("fsdp"), lax.axis_index("sub")
    swap = [(0, 1), (1, 0)]

    def to_core(a):
        return lax.ppermute(a, "sub", swap)

    def from_chip(a, d):
        return lax.ppermute(a, "fsdp", [((i + d) % chips, i) for i in range(chips)])

    far_in = [from_chip(proj_in, d) for d in range(1, chips)]
    far_out = [from_chip(proj_out, d) for d in range(1, chips)]
    near = jnp.stack([2 * x + core, 2 * x + 1 - core]).astype(jnp.int32)
    far = jnp.stack(
        [2 * ((x + d) % chips) + c for d in range(1, chips) for c in (core, 1 - core)]
    ).astype(jnp.int32)
    in_t = project(near, activations, [proj_in, to_core(proj_in)], None)
    out_t = project(near, out_grads, [proj_out, to_core(proj_out)], None)
    in_t = project(far, activations, [b for a in far_in for b in (a, to_core(a))], in_t)
    out_t = project(far, out_grads, [b for a in far_out for b in (a, to_core(a))], out_t)
    everyone = gather_queries(queries, core, sizes["traj"])
    return finish(in_t, out_t, segments, loss_mask, everyone).T


def solution(mesh):
    placed = (
        P(("groups", "traj", "fsdp", "sub"), None),
        P(("groups", "traj", "fsdp", "sub"), None),
        P(("groups", "traj", "fsdp", "sub"), None),
        P(("groups", "traj", "fsdp", "sub"), None),
        P(None, ("fsdp", "sub")),
        P(None, ("fsdp", "sub")),
        P(("groups", "traj"), None),
    )
    sizes = dict(mesh.shape)

    def program(*arrays):
        return body(sizes, *arrays)

    return jax.shard_map(
        program,
        mesh=mesh,
        in_specs=placed,
        out_specs=P("groups", ("traj", "fsdp", "sub")),
        check_vma=False,
    )
```

```python
import jax
import jax.numpy as jnp
from jax import lax
from jax.experimental import pallas as pl
from jax.experimental.pallas import tpu as pltpu
from jax.sharding import PartitionSpec as P

TRAJ_DEV = 8
NT = (((1,), (1,)), ((), ()))
ANY = pl.BlockSpec(memory_space=pl.ANY)
VMEM = pl.BlockSpec(memory_space=pltpu.VMEM)
SMEM = pl.BlockSpec(memory_space=pltpu.SMEM)
SMALL = pltpu.CompilerParams(vmem_limit_bytes=8 << 20)
PARAMS = pltpu.CompilerParams(vmem_limit_bytes=52 << 20)


def dot_nt(a, b):
    return lax.dot_general(a, b, NT, preferred_element_type=jnp.float32)


def halves(a):
    high = a.astype(jnp.bfloat16)
    return high, (a - high.astype(jnp.float32)).astype(jnp.bfloat16)


class Chunks:
    def __init__(self, toks_hbm, owner_ref, projs_hbm, toks, projs, sems, first):
        width = projs.shape[2]
        self.toks, self.projs, self.first, self.copies = toks, projs, first, []
        for i, proj in enumerate(projs_hbm):
            k = first + i
            columns = pl.ds(pl.multiple_of(owner_ref[i] * width, 128), width)
            pair = (
                pltpu.make_async_copy(proj, projs.at[k], sems.at[0, k]),
                pltpu.make_async_copy(toks_hbm.at[:, columns], toks.at[k], sems.at[1, k]),
            )
            for copy in pair:
                copy.start()
            self.copies.append(pair)

    def total(self, base):
        for i, pair in enumerate(self.copies):
            for copy in pair:
                copy.wait()
            part = dot_nt(self.toks[self.first + i], self.projs[self.first + i])
            base = part if base is None else base + part
        return base


def chunk_scratch(n, toks, projs):
    rank, width = projs[0].shape
    return [
        pltpu.VMEM((n, toks.shape[0], width), toks.dtype),
        pltpu.VMEM((n, rank, width), projs[0].dtype),
        pltpu.SemaphoreType.DMA((2, n)),
    ]


def project(acts, grads, in_owners, in_projs, out_owners, out_projs, bases):
    rank = in_projs[0].shape[0]
    count = acts.shape[0]
    n, m = len(in_projs), len(out_projs)

    def kernel(in_owner_ref, out_owner_ref, act, grad, *refs):
        proj_hbm, base_refs, refs = refs[: n + m], refs[n + m : -5], refs[-5:]
        in_ref, out_ref, *scratch = refs
        ins = Chunks(act, in_owner_ref, proj_hbm[:n], *scratch, 0)
        outs = Chunks(grad, out_owner_ref, proj_hbm[n:], *scratch, n)
        in_ref[...] = ins.total(base_refs[0][...] if bases else None)
        out_ref[...] = outs.total(base_refs[1][...] if bases else None)

    sums = jax.ShapeDtypeStruct((count, rank), jnp.float32)
    return pl.pallas_call(
        kernel,
        out_shape=(sums, sums),
        in_specs=[SMEM] * 2 + [ANY] * (2 + n + m) + [VMEM] * len(bases),
        out_specs=(VMEM, VMEM),
        scratch_shapes=chunk_scratch(n + m, acts, in_projs),
        compiler_params=PARAMS,
        cost_estimate=cost(),
    )(in_owners, out_owners, acts, grads, *in_projs, *out_projs, *bases)


def partial_scores(queries, f_stack):
    q_high, q_low = halves(queries)
    both = dot_nt(f_stack, q_high)
    return both[:TRAJ_DEV] + both[TRAJ_DEV:] + dot_nt(f_stack, q_low)[:TRAJ_DEV]


def spread_blocks(scores, places, slots):
    rows = scores.shape[1] // len(places)
    block = lax.broadcasted_iota(jnp.int32, (TRAJ_DEV, rows * slots), 1) // rows
    ordered = jnp.zeros((TRAJ_DEV, rows * slots), jnp.float32)
    for s, place in enumerate(places):
        piece = scores[:, s * rows : (s + 1) * rows]
        ordered = jnp.where(block == place, jnp.concatenate([piece] * slots, axis=1), ordered)
    return ordered


def gradients(
    acts, grads, in_owners, in_projs, out_owners, out_projs, bases, segments, loss_mask, places, pieces, slots
):
    count, rank = bases[0].shape
    rows, flat_width = pieces[0].shape
    n, m, k = len(in_projs), len(out_projs), len(pieces)

    def kernel(in_owner_ref, out_owner_ref, place_ref, act, grad, *refs):
        proj_hbm, piece_hbm, refs = refs[: n + m], refs[n + m : n + m + k], refs[n + m + k :]
        in_base, out_base, seg_ref, mask_ref, stack_ref, score_ref = refs[:6]
        *scratch, blocks, block_sems = refs[6:]
        ins = Chunks(act, in_owner_ref, proj_hbm[:n], *scratch, 0)
        outs = Chunks(grad, out_owner_ref, proj_hbm[n:], *scratch, n)
        copies = [
            pltpu.make_async_copy(piece, blocks.at[pl.ds(i * rows, rows)], block_sems.at[i])
            for i, piece in enumerate(piece_hbm)
        ]
        for copy in copies:
            copy.start()
        own = seg_ref[...] == lax.broadcasted_iota(jnp.int32, (TRAJ_DEV, count), 0)
        masked = jnp.where(own, mask_ref[...].astype(jnp.float32), 0.0)
        counts = jnp.sum(masked, axis=1, keepdims=True)
        weight = masked * (1.0 / jnp.maximum(counts, 1.0))
        in_t = ins.total(in_base[...]).T
        t_high, t_low = halves(jnp.concatenate([in_t, in_t], axis=0))
        out_t = outs.total(out_base[...]).T
        left = (out_t[:, None, :] * weight[None]).reshape(rank * TRAJ_DEV, count)
        l_high, l_low = halves(left)
        outer = dot_nt(
            jnp.concatenate([l_high, l_low], axis=1), jnp.concatenate([t_high, t_high], axis=1)
        ) + dot_nt(l_high, t_low)
        outer = outer.reshape(rank // 2, 2, TRAJ_DEV, 2 * rank)
        low = lax.broadcasted_iota(jnp.int32, (TRAJ_DEV, 2 * rank), 1) < rank
        flat = jnp.concatenate(
            [jnp.where(low, outer[p, 0], outer[p, 1]) for p in range(rank // 2)], axis=1
        )
        f_stack = jnp.concatenate(halves(flat), axis=0)
        for copy in copies:
            copy.wait()
        scores = partial_scores(blocks[...], f_stack)
        stack_ref[...] = f_stack
        score_ref[...] = spread_blocks(scores, [place_ref[s] for s in range(k)], slots)

    return pl.pallas_call(
        kernel,
        out_shape=(
            jax.ShapeDtypeStruct((2 * TRAJ_DEV, flat_width), jnp.bfloat16),
            jax.ShapeDtypeStruct((TRAJ_DEV, rows * slots), jnp.float32),
        ),
        in_specs=[SMEM] * 3 + [ANY] * (2 + n + m + k) + [VMEM] * 4,
        out_specs=(VMEM, VMEM),
        scratch_shapes=chunk_scratch(n + m, acts, in_projs)
        + [pltpu.VMEM((k * rows, flat_width), jnp.float32), pltpu.SemaphoreType.DMA((k,))],
        compiler_params=PARAMS,
        cost_estimate=cost(),
    )(
        in_owners,
        out_owners,
        places,
        acts,
        grads,
        *in_projs,
        *out_projs,
        *pieces,
        *bases,
        segments,
        loss_mask,
    )


def last_block(places, scores, f_stack, here, there):
    slots = scores.shape[1] // here.shape[0]
    at = places.shape[0] - 2

    def kernel(place_ref, base_ref, stack_ref, here_ref, there_ref, score_ref):
        block = jnp.where(place_ref[at + 1] == 0, here_ref[...], there_ref[...])
        scores = partial_scores(block, stack_ref[...])
        score_ref[...] = base_ref[...] + spread_blocks(scores, [place_ref[at]], slots)

    return pl.pallas_call(
        kernel,
        out_shape=jax.ShapeDtypeStruct(scores.shape, jnp.float32),
        in_specs=[SMEM] + [VMEM] * 4,
        out_specs=VMEM,
        compiler_params=SMALL,
        cost_estimate=cost(),
    )(places, scores, f_stack, here, there)


def cost():
    return pl.CostEstimate(flops=1, bytes_accessed=1, transcendentals=0)


def fetch_queries(queries, sizes):
    n = sizes["traj"]
    if n != 4:
        return [lax.all_gather(queries, "traj", axis=0, tiled=True)]
    line = range(n)
    beside = lax.ppermute(
        queries,
        ("traj", "sub"),
        [(2 * ((z + 1) % n), 2 * z) for z in line]
        + [(2 * ((z + n - 1) % n) + 1, 2 * z + 1) for z in line],
    )
    across = lax.ppermute(queries, ("traj", "sub"), [(2 * ((z + 2) % n), 2 * z) for z in line])
    return [beside, across]


def query_places(at, core):
    step = jnp.where(core == 0, 1, 3)
    places = jnp.stack([at, (at + step) % 4, (at + 4 - step) % 4, (at + 2) % 4, core])
    return places.astype(jnp.int32)


def body(sizes, activations, out_grads, segments, loss_mask, proj_in, proj_out, queries):
    chips = sizes["fsdp"]
    x, core = lax.axis_index("fsdp"), lax.axis_index("sub")

    def to_core(a):
        return lax.ppermute(a, "sub", [(0, 1), (1, 0)])

    def from_chip(a, d):
        return lax.ppermute(a, "fsdp", [((i + d) % chips, i) for i in range(chips)])

    def after(arrays, *waited):
        return lax.optimization_barrier((arrays, *waited))

    def numbers(*owners):
        return jnp.stack(owners).astype(jnp.int32)

    far_in = [from_chip(proj_in, d) for d in range(1, chips)]
    far_out = [from_chip(proj_out, d) for d in range(1, chips)]
    fetched = fetch_queries(queries, sizes)
    own, other = 2 * x + core, 2 * x + 1 - core
    far_own = [2 * ((x + d) % chips) + core for d in range(1, chips)]
    far_other = [2 * ((x + d) % chips) + 1 - core for d in range(1, chips)]

    places = query_places(lax.axis_index("traj"), core)
    sums = project(
        activations,
        out_grads,
        numbers(own, other),
        [proj_in, to_core(proj_in)],
        numbers(own),
        [proj_out],
        [],
    )
    (far_in, far_out, late_out), sums = after((far_in, far_out, proj_out), sums)
    others_in = [to_core(a) for a in far_in]
    others_out = [to_core(a) for a in far_out] + [to_core(late_out)]
    on_line = len(fetched) > 1
    if on_line:
        beside, across = fetched
        pieces = [queries, beside, to_core(beside)]
    else:
        pieces, places = fetched, jnp.zeros((1,), jnp.int32)
    sums = project(
        activations, out_grads, numbers(*far_own), far_in, numbers(*far_own), far_out, sums
    )
    if on_line:
        across, sums = after(across, sums)
        across_other = to_core(across)
    f_stack, scores = gradients(
        activations,
        out_grads,
        numbers(*far_other),
        others_in,
        numbers(*far_other, other),
        others_out,
        sums,
        segments,
        loss_mask,
        places,
        pieces,
        4 if on_line else 1,
    )
    if on_line:
        scores = last_block(places, scores, f_stack, across, across_other)
    return scores.T


def solution(mesh):
    placed = (
        P(("groups", "traj", "fsdp", "sub"), None),
        P(("groups", "traj", "fsdp", "sub"), None),
        P(("groups", "traj", "fsdp", "sub"), None),
        P(("groups", "traj", "fsdp", "sub"), None),
        P(None, ("fsdp", "sub")),
        P(None, ("fsdp", "sub")),
        P(("groups", "traj"), None),
    )
    sizes = dict(mesh.shape)

    def program(*arrays):
        return body(sizes, *arrays)

    return jax.shard_map(
        program,
        mesh=mesh,
        in_specs=placed,
        out_specs=P("groups", ("traj", "fsdp", "sub")),
        check_vma=False,
    )
```

```python
import jax
import jax.numpy as jnp
from jax import lax
from jax.experimental import pallas as pl
from jax.experimental.pallas import tpu as pltpu
from jax.sharding import PartitionSpec as P

TRAJ_DEV = 8
NT = (((1,), (1,)), ((), ()))
ANY = pl.BlockSpec(memory_space=pl.ANY)
VMEM = pl.BlockSpec(memory_space=pltpu.VMEM)
SMALL = pltpu.CompilerParams(vmem_limit_bytes=8 << 20)
PARAMS = pltpu.CompilerParams(vmem_limit_bytes=52 << 20)


def dot_nt(a, b):
    return lax.dot_general(a, b, NT, preferred_element_type=jnp.float32)


def halves(a):
    high = a.astype(jnp.bfloat16)
    return high, (a - high.astype(jnp.float32)).astype(jnp.bfloat16)


class Chunks:
    def __init__(self, toks_hbm, owners, projs, toks, sems, first):
        self.toks, self.projs, self.first, self.copies = toks, projs, first, []
        width = toks.shape[2]
        for i, owner in enumerate(owners):
            columns = pl.ds(pl.multiple_of(owner * width, 128), width)
            copy = pltpu.make_async_copy(
                toks_hbm.at[:, columns], toks.at[first + i], sems.at[first + i]
            )
            copy.start()
            self.copies.append(copy)

    def total(self, base):
        for i, copy in enumerate(self.copies):
            copy.wait()
            part = dot_nt(self.toks[self.first + i], self.projs[i][...])
            base = part if base is None else base + part
        return base


def chunk_scratch(n, toks, projs):
    return [
        pltpu.VMEM((n, toks.shape[0], projs[0].shape[1]), toks.dtype),
        pltpu.SemaphoreType.DMA((n,)),
    ]


def project(sides, table, bases):
    rank, width = sides[0][1][0].shape
    count = sides[0][0].shape[0]
    n, total = len(sides), sum(len(projs) for _, projs, _ in sides)

    def kernel(*refs):
        table_ref = table()
        toks, refs = refs[:n], refs[n:]
        proj_hbm, refs = refs[:total], refs[total:]
        base_refs, refs = refs[: len(bases)], refs[len(bases) :]
        out_refs, scratch = refs[:n], refs[n:]
        first, chunks = 0, []
        for tok, (_, projs, places) in zip(toks, sides):
            last = first + len(projs)
            owners = [table_ref[place] for place in places]
            chunks.append(Chunks(tok, owners, proj_hbm[first:last], *scratch, first))
            first = last
        for i, (chunk, out_ref) in enumerate(zip(chunks, out_refs)):
            out_ref[...] = chunk.total(base_refs[i][...] if i < len(bases) else None)

    shapes = [jax.ShapeDtypeStruct((count, rank), jnp.float32)] * n
    scratch = chunk_scratch(total, sides[0][0], sides[0][1])
    return pl.pallas_call(
        kernel,
        out_shape=shapes,
        in_specs=[ANY] * n + [VMEM] * (total + len(bases)),
        out_specs=[VMEM] * n,
        scratch_shapes=scratch,
        compiler_params=PARAMS,
        cost_estimate=cost(),
    )(*[side[0] for side in sides], *[p for side in sides for p in side[1]], *bases)


def partial_scores(q_halves, f_stack):
    q_high, q_low = q_halves
    both = dot_nt(f_stack, q_high)
    return both[:TRAJ_DEV] + both[TRAJ_DEV:] + dot_nt(f_stack, q_low)[:TRAJ_DEV]


def spread_blocks(scores, places, slots):
    rows = scores.shape[1] // len(places)
    block = lax.broadcasted_iota(jnp.int32, (TRAJ_DEV, rows * slots), 1) // rows
    ordered = jnp.zeros((TRAJ_DEV, rows * slots), jnp.float32)
    for s, place in enumerate(places):
        piece = scores[:, s * rows : (s + 1) * rows]
        ordered = jnp.where(block == place, jnp.concatenate([piece] * slots, axis=1), ordered)
    return ordered


def gradients(
    table, in_side, out_side, bases, segments, loss_mask, numbered, pieces, slots
):
    count, rank = bases[0].shape
    rows, flat_width = pieces[0].shape
    acts, in_projs, in_places = in_side
    grads, out_projs, out_places = out_side
    n, m, k = len(in_projs), len(out_projs), len(pieces)

    def kernel(act, grad, *refs):
        table_ref = table()
        proj_hbm, piece_refs, refs = refs[: n + m], refs[n + m : n + m + k], refs[n + m + k :]
        in_base, out_base, seg_ref, mask_ref, stack_ref, score_ref = refs[:6]
        scratch = refs[6:]
        ins = Chunks(act, [table_ref[p] for p in in_places], proj_hbm[:n], *scratch, 0)
        outs = Chunks(grad, [table_ref[p] for p in out_places], proj_hbm[n:], *scratch, n)
        q_halves = halves(jnp.concatenate([ref[...] for ref in piece_refs], axis=0))
        own = seg_ref[...] == lax.broadcasted_iota(jnp.int32, (TRAJ_DEV, count), 0)
        masked = jnp.where(own, mask_ref[...].astype(jnp.float32), 0.0)
        counts = jnp.sum(masked, axis=1, keepdims=True)
        weight = masked * (1.0 / jnp.maximum(counts, 1.0))
        in_t = ins.total(in_base[...]).T
        t_high, t_low = halves(jnp.concatenate([in_t, in_t], axis=0))
        out_t = outs.total(out_base[...]).T
        left = (out_t[:, None, :] * weight[None]).reshape(rank * TRAJ_DEV, count)
        l_high, l_low = halves(left)
        outer = dot_nt(
            jnp.concatenate([l_high, l_low], axis=1), jnp.concatenate([t_high, t_high], axis=1)
        ) + dot_nt(l_high, t_low)
        outer = outer.reshape(rank // 2, 2, TRAJ_DEV, 2 * rank)
        low = lax.broadcasted_iota(jnp.int32, (TRAJ_DEV, 2 * rank), 1) < rank
        flat = jnp.concatenate(
            [jnp.where(low, outer[p, 0], outer[p, 1]) for p in range(rank // 2)], axis=1
        )
        f_stack = jnp.concatenate(halves(flat), axis=0)
        scores = partial_scores(q_halves, f_stack)
        stack_ref[...] = f_stack
        score_ref[...] = spread_blocks(scores, [table_ref[p] for p in numbered], slots)

    return pl.pallas_call(
        kernel,
        out_shape=(
            jax.ShapeDtypeStruct((2 * TRAJ_DEV, flat_width), jnp.bfloat16),
            jax.ShapeDtypeStruct((TRAJ_DEV, rows * slots), jnp.float32),
        ),
        in_specs=[ANY] * 2 + [VMEM] * (n + m + k + 4),
        out_specs=(VMEM, VMEM),
        scratch_shapes=chunk_scratch(n + m, acts, in_projs),
        compiler_params=PARAMS,
        cost_estimate=cost(),
    )(
        acts,
        grads,
        *in_projs,
        *out_projs,
        *pieces,
        *bases,
        segments,
        loss_mask,
    )


def last_block(table, numbered, scores, f_stack, here, there):
    slots = scores.shape[1] // here.shape[0]

    def kernel(base_ref, stack_ref, here_ref, there_ref, score_ref):
        table_ref = table()
        block = jnp.where(table_ref[numbered[1]] == 0, here_ref[...], there_ref[...])
        scores = partial_scores(halves(block), stack_ref[...])
        score_ref[...] = base_ref[...] + spread_blocks(scores, [table_ref[numbered[0]]], slots)

    return pl.pallas_call(
        kernel,
        out_shape=jax.ShapeDtypeStruct(scores.shape, jnp.float32),
        in_specs=[VMEM] * 4,
        out_specs=VMEM,
        compiler_params=SMALL,
        cost_estimate=cost(),
    )(scores, f_stack, here, there)


def cost():
    return pl.CostEstimate(flops=1, bytes_accessed=1, transcendentals=0)


def fetch_queries(queries, sizes):
    n = sizes["traj"]
    if n != 4:
        return [lax.all_gather(queries, "traj", axis=0, tiled=True)]
    line = range(n)
    beside = lax.ppermute(
        queries,
        ("traj", "sub"),
        [(2 * ((z + 1) % n), 2 * z) for z in line]
        + [(2 * ((z + n - 1) % n) + 1, 2 * z + 1) for z in line],
    )
    across = lax.ppermute(queries, ("traj", "sub"), [(2 * ((z + 2) % n), 2 * z) for z in line])
    return [beside, across]


def body(sizes, activations, out_grads, segments, loss_mask, proj_in, proj_out, queries):
    chips = sizes["fsdp"]

    def to_core(a):
        return lax.ppermute(a, "sub", [(0, 1), (1, 0)])

    def from_chip(a, d):
        return lax.ppermute(a, "fsdp", [((i + d) % chips, i) for i in range(chips)])

    def after(arrays, *waited):
        return lax.optimization_barrier((arrays, *waited))

    far_in = [from_chip(proj_in, d) for d in range(1, chips)]
    far_out = [from_chip(proj_out, d) for d in range(1, chips)]
    fetched = fetch_queries(queries, sizes)
    on_line = len(fetched) > 1

    far_own, far_other = [2 * d for d in range(1, chips)], [2 * d + 1 for d in range(1, chips)]
    numbered = [2 * chips + s for s in range(5)]

    def table():
        x, core = lax.axis_index("fsdp"), lax.axis_index("sub")
        chunks = [2 * lax.rem(x + d, chips) + c for d in range(chips) for c in (core, 1 - core)]
        if not on_line:
            return chunks + [0]
        at, step = lax.axis_index("traj"), 1 + 2 * core
        blocks = [at, at + step, at + 4 - step, at + 2]
        return chunks + [lax.rem(b, 4) for b in blocks] + [core]

    in_sum, out_sum = project(
        [(activations, [proj_in, to_core(proj_in)], [0, 1]), (out_grads, [proj_out], [0])],
        table,
        [],
    )
    far_in, late_out, in_sum, out_sum = after(far_in, proj_out, in_sum, out_sum)
    others_in = [to_core(a) for a in far_in]
    other_out = to_core(late_out)
    (in_sum,) = project([(activations, far_in, far_own)], table, [in_sum])
    if on_line:
        beside, across = fetched
        beside, in_sum = after(beside, in_sum)
        beside_other = to_core(beside)
    else:
        pieces = fetched
    far_out, beside, in_sum = after(far_out, beside if on_line else in_sum, in_sum)
    others_out = [to_core(a) for a in far_out] + [other_out]
    if on_line:
        pieces = [queries, beside, beside_other]
    (out_sum,) = project([(out_grads, far_out, far_own)], table, [out_sum])
    if on_line:
        across, out_sum = after(across, out_sum)
        across_other = to_core(across)
    f_stack, scores = gradients(
        table,
        (activations, others_in, far_other),
        (out_grads, others_out, far_other + [1]),
        (in_sum, out_sum),
        segments,
        loss_mask,
        numbered[: len(pieces)],
        pieces,
        4 if on_line else 1,
    )
    if on_line:
        scores = last_block(table, numbered[3:], scores, f_stack, across, across_other)
    return scores.T


def solution(mesh):
    placed = (
        P(("groups", "traj", "fsdp", "sub"), None),
        P(("groups", "traj", "fsdp", "sub"), None),
        P(("groups", "traj", "fsdp", "sub"), None),
        P(("groups", "traj", "fsdp", "sub"), None),
        P(None, ("fsdp", "sub")),
        P(None, ("fsdp", "sub")),
        P(("groups", "traj"), None),
    )
    sizes = dict(mesh.shape)

    def program(*arrays):
        return body(sizes, *arrays)

    return jax.shard_map(
        program,
        mesh=mesh,
        in_specs=placed,
        out_specs=P("groups", ("traj", "fsdp", "sub")),
        check_vma=False,
    )
```

```python
import jax
import jax.numpy as jnp
from jax import lax
from jax.experimental import pallas as pl
from jax.experimental.pallas import tpu as pltpu
from jax.sharding import PartitionSpec as P

TRAJ_DEV = 8
NT = (((1,), (1,)), ((), ()))
ANY = pl.BlockSpec(memory_space=pl.ANY)
VMEM = pl.BlockSpec(memory_space=pltpu.VMEM)
SMALL = pltpu.CompilerParams(vmem_limit_bytes=8 << 20)
PARAMS = pltpu.CompilerParams(vmem_limit_bytes=52 << 20)


def dot_nt(a, b):
    return lax.dot_general(a, b, NT, preferred_element_type=jnp.float32)


def halves(a):
    high = a.astype(jnp.bfloat16)
    return high, (a - high.astype(jnp.float32)).astype(jnp.bfloat16)


class Chunks:
    def __init__(self, toks_hbm, owners, projs, toks, sems, first):
        self.toks, self.projs, self.first, self.copies = toks, projs, first, []
        width = toks.shape[2]
        for i, owner in enumerate(owners):
            columns = pl.ds(pl.multiple_of(owner * width, 128), width)
            copy = pltpu.make_async_copy(
                toks_hbm.at[:, columns], toks.at[first + i], sems.at[first + i]
            )
            copy.start()
            self.copies.append(copy)

    def total(self, base):
        for i, copy in enumerate(self.copies):
            copy.wait()
            part = dot_nt(self.toks[self.first + i], self.projs[i][...])
            base = part if base is None else base + part
        return base


def chunk_scratch(n, toks, projs):
    return [
        pltpu.VMEM((n, toks.shape[0], projs[0].shape[1]), toks.dtype),
        pltpu.SemaphoreType.DMA((n,)),
    ]


def project(sides, table, bases):
    rank, width = sides[0][1][0].shape
    count = sides[0][0].shape[0]
    n, total = len(sides), sum(len(projs) for _, projs, _ in sides)

    def kernel(*refs):
        table_ref = table()
        toks, refs = refs[:n], refs[n:]
        proj_hbm, refs = refs[:total], refs[total:]
        base_refs, refs = refs[: len(bases)], refs[len(bases) :]
        out_refs, scratch = refs[:n], refs[n:]
        first, chunks = 0, []
        for tok, (_, projs, places) in zip(toks, sides):
            last = first + len(projs)
            owners = [table_ref[place] for place in places]
            chunks.append(Chunks(tok, owners, proj_hbm[first:last], *scratch, first))
            first = last
        for i, (chunk, out_ref) in enumerate(zip(chunks, out_refs)):
            out_ref[...] = chunk.total(base_refs[i][...] if i < len(bases) else None)

    shapes = [jax.ShapeDtypeStruct((count, rank), jnp.float32)] * n
    scratch = chunk_scratch(total, sides[0][0], sides[0][1])
    return pl.pallas_call(
        kernel,
        out_shape=shapes,
        in_specs=[ANY] * n + [VMEM] * (total + len(bases)),
        out_specs=[VMEM] * n,
        scratch_shapes=scratch,
        compiler_params=PARAMS,
        cost_estimate=cost(),
    )(*[side[0] for side in sides], *[p for side in sides for p in side[1]], *bases)


def add_chunks(base, toks, projs):
    n = len(toks)

    def kernel(base_ref, *refs):
        total = base_ref[...]
        for tok, proj in zip(refs[:n], refs[n : 2 * n]):
            total = total + dot_nt(tok[...], proj[...])
        refs[2 * n][...] = total

    return pl.pallas_call(
        kernel,
        out_shape=jax.ShapeDtypeStruct(base.shape, base.dtype),
        in_specs=[VMEM] * (1 + 2 * n),
        out_specs=VMEM,
        compiler_params=SMALL,
        cost_estimate=cost(),
    )(base, *toks, *projs)


def partial_scores(q_halves, f_stack):
    q_high, q_low = q_halves
    both = dot_nt(f_stack, q_high)
    return both[:TRAJ_DEV] + both[TRAJ_DEV:] + dot_nt(f_stack, q_low)[:TRAJ_DEV]


def spread_blocks(scores, places, slots):
    rows = scores.shape[1] // len(places)
    block = lax.broadcasted_iota(jnp.int32, (TRAJ_DEV, rows * slots), 1) // rows
    ordered = jnp.zeros((TRAJ_DEV, rows * slots), jnp.float32)
    for s, place in enumerate(places):
        piece = scores[:, s * rows : (s + 1) * rows]
        ordered = jnp.where(block == place, jnp.concatenate([piece] * slots, axis=1), ordered)
    return ordered


def gradients(
    table, in_side, out_side, bases, segments, loss_mask, numbered, pieces, slots
):
    count, rank = bases[0].shape
    rows, flat_width = pieces[0].shape
    acts, in_projs = in_side
    grads, out_projs = out_side
    n, m, k = len(in_projs), len(out_projs), len(pieces)

    def kernel(*refs):
        table_ref = table()
        tok_refs, refs = refs[: n + m], refs[n + m :]
        proj_refs, piece_refs, refs = refs[: n + m], refs[n + m : n + m + k], refs[n + m + k :]
        parts = [dot_nt(tok[...], proj[...]) for tok, proj in zip(tok_refs, proj_refs)]
        in_base, out_base, seg_ref, mask_ref, stack_ref, score_ref = refs
        q_halves = halves(jnp.concatenate([ref[...] for ref in piece_refs], axis=0))
        own = seg_ref[...] == lax.broadcasted_iota(jnp.int32, (TRAJ_DEV, count), 0)
        masked = jnp.where(own, mask_ref[...].astype(jnp.float32), 0.0)
        counts = jnp.sum(masked, axis=1, keepdims=True)
        weight = masked * (1.0 / jnp.maximum(counts, 1.0))
        in_t = sum(parts[:n], in_base[...]).T
        t_high, t_low = halves(jnp.concatenate([in_t, in_t], axis=0))
        out_t = sum(parts[n:], out_base[...]).T
        left = (out_t[:, None, :] * weight[None]).reshape(rank * TRAJ_DEV, count)
        l_high, l_low = halves(left)
        outer = dot_nt(
            jnp.concatenate([l_high, l_low], axis=1), jnp.concatenate([t_high, t_high], axis=1)
        ) + dot_nt(l_high, t_low)
        outer = outer.reshape(rank // 2, 2, TRAJ_DEV, 2 * rank)
        low = lax.broadcasted_iota(jnp.int32, (TRAJ_DEV, 2 * rank), 1) < rank
        flat = jnp.concatenate(
            [jnp.where(low, outer[p, 0], outer[p, 1]) for p in range(rank // 2)], axis=1
        )
        f_stack = jnp.concatenate(halves(flat), axis=0)
        scores = partial_scores(q_halves, f_stack)
        stack_ref[...] = f_stack
        score_ref[...] = spread_blocks(scores, [table_ref[p] for p in numbered], slots)

    return pl.pallas_call(
        kernel,
        out_shape=(
            jax.ShapeDtypeStruct((2 * TRAJ_DEV, flat_width), jnp.bfloat16),
            jax.ShapeDtypeStruct((TRAJ_DEV, rows * slots), jnp.float32),
        ),
        in_specs=[VMEM] * (2 * (n + m) + k + 4),
        out_specs=(VMEM, VMEM),
        compiler_params=SMALL,
        cost_estimate=cost(),
    )(
        *acts,
        *grads,
        *in_projs,
        *out_projs,
        *pieces,
        *bases,
        segments,
        loss_mask,
    )


def last_block(table, numbered, scores, f_stack, here, there):
    slots = scores.shape[1] // here.shape[0]

    def kernel(base_ref, stack_ref, here_ref, there_ref, score_ref):
        table_ref = table()
        block = jnp.where(table_ref[numbered[1]] == 0, here_ref[...], there_ref[...])
        scores = partial_scores(halves(block), stack_ref[...])
        score_ref[...] = base_ref[...] + spread_blocks(scores, [table_ref[numbered[0]]], slots)

    return pl.pallas_call(
        kernel,
        out_shape=jax.ShapeDtypeStruct(scores.shape, jnp.float32),
        in_specs=[VMEM] * 4,
        out_specs=VMEM,
        compiler_params=SMALL,
        cost_estimate=cost(),
    )(scores, f_stack, here, there)


def cost():
    return pl.CostEstimate(flops=1, bytes_accessed=1, transcendentals=0)


def fetch_queries(queries, sizes):
    n = sizes["traj"]
    if n != 4:
        return [lax.all_gather(queries, "traj", axis=0, tiled=True)]
    line = range(n)
    beside = lax.ppermute(
        queries,
        ("traj", "sub"),
        [(2 * ((z + 1) % n), 2 * z) for z in line]
        + [(2 * ((z + n - 1) % n) + 1, 2 * z + 1) for z in line],
    )
    across = lax.ppermute(queries, ("traj", "sub"), [(2 * ((z + 2) % n), 2 * z) for z in line])
    return [beside, across]


def body(sizes, activations, out_grads, segments, loss_mask, proj_in, proj_out, queries):
    chips, width = sizes["fsdp"], proj_in.shape[1]

    def to_core(a):
        return lax.ppermute(a, "sub", [(0, 1), (1, 0)])

    def from_chip(a, d):
        return lax.ppermute(a, "fsdp", [((i + d) % chips, i) for i in range(chips)])

    def after(arrays, *waited):
        return lax.optimization_barrier((arrays, *waited))

    far_in = [from_chip(proj_in, d) for d in range(1, chips)]
    far_out = [from_chip(proj_out, d) for d in range(1, chips)]
    fetched = fetch_queries(queries, sizes)
    on_line = len(fetched) > 1

    far_own, far_other = [2 * d for d in range(1, chips)], [2 * d + 1 for d in range(1, chips)]
    numbered = [2 * chips + s for s in range(5)]

    def table():
        x, core = lax.axis_index("fsdp"), lax.axis_index("sub")
        chunks = [2 * lax.rem(x + d, chips) + c for d in range(chips) for c in (core, 1 - core)]
        if not on_line:
            return chunks + [0]
        at, step = lax.axis_index("traj"), 1 + 2 * core
        blocks = [at, at + step, at + 4 - step, at + 2]
        return chunks + [lax.rem(b, 4) for b in blocks] + [core]

    in_sum, out_sum = project(
        [(activations, [proj_in, to_core(proj_in)], [0, 1]), (out_grads, [proj_out], [0])],
        table,
        [],
    )
    far_in, late_out, in_sum, out_sum = after(far_in, proj_out, in_sum, out_sum)
    others_in = [to_core(a) for a in far_in]
    other_out = to_core(late_out)
    (in_sum,) = project([(activations, far_in, far_own)], table, [in_sum])
    if on_line:
        beside, across = fetched
        beside, in_sum = after(beside, in_sum)
        beside_other = to_core(beside)
    else:
        pieces = fetched
    chunk = table()
    activations, out_grads, in_sum = after(activations, out_grads, in_sum)
    cut = [
        [
            lax.dynamic_slice_in_dim(array, chunk[place] * width, width, 1)
            for place in places
        ]
        for array, places in (
            (out_grads, far_own),
            (activations, far_other),
            (out_grads, far_other + [1]),
        )
    ]
    far_out, in_sum, cut = after(far_out, in_sum, cut)
    grads_own, acts_other, grads_other = cut
    if on_line:
        far_out, beside = after(far_out, beside)
        pieces = [queries, beside, beside_other]
    others_out = [to_core(a) for a in far_out] + [other_out]
    out_sum = add_chunks(out_sum, grads_own, far_out)
    if on_line:
        across, out_sum = after(across, out_sum)
        across_other = to_core(across)
    f_stack, scores = gradients(
        table,
        (acts_other, others_in),
        (grads_other, others_out),
        (in_sum, out_sum),
        segments,
        loss_mask,
        numbered[: len(pieces)],
        pieces,
        4 if on_line else 1,
    )
    if on_line:
        scores = last_block(table, numbered[3:], scores, f_stack, across, across_other)
    return scores.T


def solution(mesh):
    placed = (
        P(("groups", "traj", "fsdp", "sub"), None),
        P(("groups", "traj", "fsdp", "sub"), None),
        P(("groups", "traj", "fsdp", "sub"), None),
        P(("groups", "traj", "fsdp", "sub"), None),
        P(None, ("fsdp", "sub")),
        P(None, ("fsdp", "sub")),
        P(("groups", "traj"), None),
    )
    sizes = dict(mesh.shape)

    def program(*arrays):
        return body(sizes, *arrays)

    return jax.shard_map(
        program,
        mesh=mesh,
        in_specs=placed,
        out_specs=P("groups", ("traj", "fsdp", "sub")),
        check_vma=False,
    )
```

```python
import jax
import jax.numpy as jnp
from jax import lax
from jax.experimental import pallas as pl
from jax.experimental.pallas import tpu as pltpu
from jax.sharding import PartitionSpec as P

TRAJ_DEV = 8
NT = (((1,), (1,)), ((), ()))
ANY = pl.BlockSpec(memory_space=pl.ANY)
VMEM = pl.BlockSpec(memory_space=pltpu.VMEM)
SMALL = pltpu.CompilerParams(vmem_limit_bytes=8 << 20)
PARAMS = pltpu.CompilerParams(vmem_limit_bytes=52 << 20)


def dot_nt(a, b):
    return lax.dot_general(a, b, NT, preferred_element_type=jnp.float32)


def halves(a):
    high = a.astype(jnp.bfloat16)
    return high, (a - high.astype(jnp.float32)).astype(jnp.bfloat16)


class Chunks:
    def __init__(self, toks_hbm, owners, projs, toks, sems, first):
        self.toks, self.projs, self.first, self.copies = toks, projs, first, []
        width = toks.shape[2]
        for i, owner in enumerate(owners):
            columns = pl.ds(pl.multiple_of(owner * width, 128), width)
            copy = pltpu.make_async_copy(
                toks_hbm.at[:, columns], toks.at[first + i], sems.at[first + i]
            )
            copy.start()
            self.copies.append(copy)

    def total(self, base):
        for i, copy in enumerate(self.copies):
            copy.wait()
            part = dot_nt(self.toks[self.first + i], self.projs[i][...])
            base = part if base is None else base + part
        return base


def chunk_scratch(n, toks, projs):
    return [
        pltpu.VMEM((n, toks.shape[0], projs[0].shape[1]), toks.dtype),
        pltpu.SemaphoreType.DMA((n,)),
    ]


def project(sides, table, bases):
    rank, width = sides[0][1][0].shape
    count = sides[0][0].shape[0]
    n, total = len(sides), sum(len(projs) for _, projs, _ in sides)

    def kernel(*refs):
        table_ref = table()
        toks, refs = refs[:n], refs[n:]
        proj_hbm, refs = refs[:total], refs[total:]
        base_refs, refs = refs[: len(bases)], refs[len(bases) :]
        out_refs, scratch = refs[:n], refs[n:]
        first, chunks = 0, []
        for tok, (_, projs, places) in zip(toks, sides):
            last = first + len(projs)
            owners = [table_ref[place] for place in places]
            chunks.append(Chunks(tok, owners, proj_hbm[first:last], *scratch, first))
            first = last
        for i, (chunk, out_ref) in enumerate(zip(chunks, out_refs)):
            out_ref[...] = chunk.total(base_refs[i][...] if i < len(bases) else None)

    shapes = [jax.ShapeDtypeStruct((count, rank), jnp.float32)] * n
    scratch = chunk_scratch(total, sides[0][0], sides[0][1])
    return pl.pallas_call(
        kernel,
        out_shape=shapes,
        in_specs=[ANY] * n + [VMEM] * (total + len(bases)),
        out_specs=[VMEM] * n,
        scratch_shapes=scratch,
        compiler_params=PARAMS,
        cost_estimate=cost(),
    )(*[side[0] for side in sides], *[p for side in sides for p in side[1]], *bases)


def add_chunks(base, toks, projs):
    n = len(toks)

    def kernel(base_ref, *refs):
        total = base_ref[...]
        for tok, proj in zip(refs[:n], refs[n : 2 * n]):
            total = total + dot_nt(tok[...], proj[...])
        refs[2 * n][...] = total

    return pl.pallas_call(
        kernel,
        out_shape=jax.ShapeDtypeStruct(base.shape, base.dtype),
        in_specs=[VMEM] * (1 + 2 * n),
        out_specs=VMEM,
        compiler_params=SMALL,
        cost_estimate=cost(),
    )(base, *toks, *projs)


def partial_scores(q_halves, f_stack):
    q_high, q_low = q_halves
    both = dot_nt(f_stack, q_high)
    return both[:TRAJ_DEV] + both[TRAJ_DEV:] + dot_nt(f_stack, q_low)[:TRAJ_DEV]


def spread_blocks(scores, places, slots):
    rows = scores.shape[1] // len(places)
    block = lax.broadcasted_iota(jnp.int32, (TRAJ_DEV, rows * slots), 1) // rows
    ordered = jnp.zeros((TRAJ_DEV, rows * slots), jnp.float32)
    for s, place in enumerate(places):
        piece = scores[:, s * rows : (s + 1) * rows]
        ordered = jnp.where(block == place, jnp.concatenate([piece] * slots, axis=1), ordered)
    return ordered


def gradients(
    table, in_side, out_side, bases, segments, loss_mask, numbered, pieces, slots
):
    count, rank = bases[0].shape
    rows, flat_width = pieces[0].shape
    acts, in_projs = in_side
    grads, out_projs = out_side
    n, m, k = len(in_projs), len(out_projs), len(pieces)

    def kernel(*refs):
        table_ref = table()
        tok_refs, refs = refs[: n + m], refs[n + m :]
        proj_refs, piece_refs, refs = refs[: n + m], refs[n + m : n + m + k], refs[n + m + k :]
        parts = [dot_nt(tok[...], proj[...]) for tok, proj in zip(tok_refs, proj_refs)]
        in_base, out_base, seg_ref, mask_ref, stack_ref, score_ref = refs
        q_halves = halves(jnp.concatenate([ref[...] for ref in piece_refs], axis=0))
        own = seg_ref[...] == lax.broadcasted_iota(jnp.int32, (TRAJ_DEV, count), 0)
        masked = jnp.where(own, mask_ref[...].astype(jnp.float32), 0.0)
        counts = jnp.sum(masked, axis=1, keepdims=True)
        weight = masked * (1.0 / jnp.maximum(counts, 1.0))
        in_t = sum(parts[:n], in_base[...]).T
        t_high, t_low = halves(jnp.concatenate([in_t, in_t], axis=0))
        out_t = sum(parts[n:], out_base[...]).T
        left = (out_t[:, None, :] * weight[None]).reshape(rank * TRAJ_DEV, count)
        l_high, l_low = halves(left)
        outer = dot_nt(
            jnp.concatenate([l_high, l_low], axis=1), jnp.concatenate([t_high, t_high], axis=1)
        ) + dot_nt(l_high, t_low)
        outer = outer.reshape(rank // 2, 2, TRAJ_DEV, 2 * rank)
        low = lax.broadcasted_iota(jnp.int32, (TRAJ_DEV, 2 * rank), 1) < rank
        flat = jnp.concatenate(
            [jnp.where(low, outer[p, 0], outer[p, 1]) for p in range(rank // 2)], axis=1
        )
        f_stack = jnp.concatenate(halves(flat), axis=0)
        scores = partial_scores(q_halves, f_stack)
        stack_ref[...] = f_stack
        score_ref[...] = spread_blocks(scores, [table_ref[p] for p in numbered], slots)

    return pl.pallas_call(
        kernel,
        out_shape=(
            jax.ShapeDtypeStruct((2 * TRAJ_DEV, flat_width), jnp.bfloat16),
            jax.ShapeDtypeStruct((TRAJ_DEV, rows * slots), jnp.float32),
        ),
        in_specs=[VMEM] * (2 * (n + m) + k + 4),
        out_specs=(VMEM, VMEM),
        compiler_params=SMALL,
        cost_estimate=cost(),
    )(
        *acts,
        *grads,
        *in_projs,
        *out_projs,
        *pieces,
        *bases,
        segments,
        loss_mask,
    )


def last_block(table, numbered, scores, f_stack, here, there):
    slots = scores.shape[1] // here.shape[0]

    def kernel(base_ref, stack_ref, here_ref, there_ref, score_ref):
        table_ref = table()
        block = jnp.where(table_ref[numbered[1]] == 0, here_ref[...], there_ref[...])
        scores = partial_scores(halves(block), stack_ref[...])
        score_ref[...] = base_ref[...] + spread_blocks(scores, [table_ref[numbered[0]]], slots)

    return pl.pallas_call(
        kernel,
        out_shape=jax.ShapeDtypeStruct(scores.shape, jnp.float32),
        in_specs=[VMEM] * 4,
        out_specs=VMEM,
        compiler_params=SMALL,
        cost_estimate=cost(),
    )(scores, f_stack, here, there)


def cost():
    return pl.CostEstimate(flops=1, bytes_accessed=1, transcendentals=0)


def fetch_queries(queries, sizes):
    n = sizes["traj"]
    if n != 4:
        return [lax.all_gather(queries, "traj", axis=0, tiled=True)]
    line = range(n)
    beside = lax.ppermute(
        queries,
        ("traj", "sub"),
        [(2 * ((z + 1) % n), 2 * z) for z in line]
        + [(2 * ((z + n - 1) % n) + 1, 2 * z + 1) for z in line],
    )
    across = lax.ppermute(queries, ("traj", "sub"), [(2 * ((z + 2) % n), 2 * z) for z in line])
    return [beside, across]


def body(sizes, activations, out_grads, segments, loss_mask, proj_in, proj_out, queries):
    chips, width = sizes["fsdp"], proj_in.shape[1]

    def to_core(a):
        return lax.ppermute(a, "sub", [(0, 1), (1, 0)])

    def from_chip(a, d):
        return lax.ppermute(a, "fsdp", [((i + d) % chips, i) for i in range(chips)])

    def after(arrays, *waited):
        return lax.optimization_barrier((arrays, *waited))

    far_in = [from_chip(proj_in, d) for d in range(1, chips)]
    far_out = [from_chip(proj_out, d) for d in range(1, chips)]
    fetched = fetch_queries(queries, sizes)
    on_line = len(fetched) > 1

    far_own, far_other = [2 * d for d in range(1, chips)], [2 * d + 1 for d in range(1, chips)]
    numbered = [2 * chips + s for s in range(5)]

    def table():
        x, core = lax.axis_index("fsdp"), lax.axis_index("sub")
        chunks = [2 * lax.rem(x + d, chips) + c for d in range(chips) for c in (core, 1 - core)]
        if not on_line:
            return chunks + [0]
        at, step = lax.axis_index("traj"), 1 + 2 * core
        blocks = [at, at + step, at + 4 - step, at + 2]
        return chunks + [lax.rem(b, 4) for b in blocks] + [core]

    in_sum, out_sum = project(
        [(activations, [proj_in], [0]), (out_grads, [proj_out], [0])],
        table,
        [],
    )
    first = fetched[:1] if on_line else []
    far_in, first, late_out, in_sum, out_sum = after(far_in, first, proj_out, in_sum, out_sum)
    fetched = first + fetched[len(first) :]
    others_in = [to_core(a) for a in far_in]
    other_out = to_core(late_out)
    (in_sum,) = project(
        [(activations, far_in + [to_core(proj_in)], far_own + [1])], table, [in_sum]
    )
    if on_line:
        beside, across = fetched
        beside_other = to_core(beside)
    else:
        pieces = fetched
    chunk = table()
    activations, out_grads, in_sum = after(activations, out_grads, in_sum)
    cut = [
        [
            lax.dynamic_slice_in_dim(array, chunk[place] * width, width, 1)
            for place in places
        ]
        for array, places in (
            (out_grads, far_own),
            (activations, far_other),
            (out_grads, far_other + [1]),
        )
    ]
    far_out, in_sum, cut = after(far_out, in_sum, cut)
    grads_own, acts_other, grads_other = cut
    if on_line:
        far_out, beside = after(far_out, beside)
        pieces = [queries, beside, beside_other]
    others_out = [to_core(a) for a in far_out] + [other_out]
    out_sum = add_chunks(out_sum, grads_own, far_out)
    if on_line:
        across, out_sum = after(across, out_sum)
        across_other = to_core(across)
    f_stack, scores = gradients(
        table,
        (acts_other, others_in),
        (grads_other, others_out),
        (in_sum, out_sum),
        segments,
        loss_mask,
        numbered[: len(pieces)],
        pieces,
        4 if on_line else 1,
    )
    if on_line:
        scores = last_block(table, numbered[3:], scores, f_stack, across, across_other)
    return scores.T


def solution(mesh):
    placed = (
        P(("groups", "traj", "fsdp", "sub"), None),
        P(("groups", "traj", "fsdp", "sub"), None),
        P(("groups", "traj", "fsdp", "sub"), None),
        P(("groups", "traj", "fsdp", "sub"), None),
        P(None, ("fsdp", "sub")),
        P(None, ("fsdp", "sub")),
        P(("groups", "traj"), None),
    )
    sizes = dict(mesh.shape)

    def program(*arrays):
        return body(sizes, *arrays)

    return jax.shard_map(
        program,
        mesh=mesh,
        in_specs=placed,
        out_specs=P("groups", ("traj", "fsdp", "sub")),
        check_vma=False,
    )
```

```python
import jax
import jax.numpy as jnp
from jax import lax
from jax.experimental import pallas as pl
from jax.experimental.pallas import tpu as pltpu
from jax.sharding import PartitionSpec as P

TRAJ_DEV = 8
NT = (((1,), (1,)), ((), ()))
ANY = pl.BlockSpec(memory_space=pl.ANY)
VMEM = pl.BlockSpec(memory_space=pltpu.VMEM)
SMALL = pltpu.CompilerParams(vmem_limit_bytes=8 << 20)
PARAMS = pltpu.CompilerParams(vmem_limit_bytes=52 << 20)


def dot_nt(a, b):
    return lax.dot_general(a, b, NT, preferred_element_type=jnp.float32)


def halves(a):
    high = a.astype(jnp.bfloat16)
    return high, (a - high.astype(jnp.float32)).astype(jnp.bfloat16)


class Chunks:
    def __init__(self, toks_hbm, owners, projs, toks, sems, first):
        self.toks, self.projs, self.first, self.copies = toks, projs, first, []
        width = toks.shape[2]
        for i, owner in enumerate(owners):
            columns = pl.ds(pl.multiple_of(owner * width, 128), width)
            copy = pltpu.make_async_copy(
                toks_hbm.at[:, columns], toks.at[first + i], sems.at[first + i]
            )
            copy.start()
            self.copies.append(copy)

    def total(self, base):
        for i, copy in enumerate(self.copies):
            copy.wait()
            part = dot_nt(self.toks[self.first + i], self.projs[i][...])
            base = part if base is None else base + part
        return base


def chunk_scratch(n, toks, projs):
    return [
        pltpu.VMEM((n, toks.shape[0], projs[0].shape[1]), toks.dtype),
        pltpu.SemaphoreType.DMA((n,)),
    ]


def project(sides, table, bases):
    rank, width = sides[0][1][0].shape
    count = sides[0][0].shape[0]
    n, total = len(sides), sum(len(projs) for _, projs, _ in sides)

    def kernel(*refs):
        table_ref = table()
        toks, refs = refs[:n], refs[n:]
        proj_hbm, refs = refs[:total], refs[total:]
        base_refs, refs = refs[: len(bases)], refs[len(bases) :]
        out_refs, scratch = refs[:n], refs[n:]
        first, chunks = 0, []
        for tok, (_, projs, places) in zip(toks, sides):
            last = first + len(projs)
            owners = [table_ref[place] for place in places]
            chunks.append(Chunks(tok, owners, proj_hbm[first:last], *scratch, first))
            first = last
        for i, (chunk, out_ref) in enumerate(zip(chunks, out_refs)):
            out_ref[...] = chunk.total(base_refs[i][...] if i < len(bases) else None)

    shapes = [jax.ShapeDtypeStruct((count, rank), jnp.float32)] * n
    scratch = chunk_scratch(total, sides[0][0], sides[0][1])
    return pl.pallas_call(
        kernel,
        out_shape=shapes,
        in_specs=[ANY] * n + [VMEM] * (total + len(bases)),
        out_specs=[VMEM] * n,
        scratch_shapes=scratch,
        compiler_params=PARAMS,
        cost_estimate=cost(),
    )(*[side[0] for side in sides], *[p for side in sides for p in side[1]], *bases)


def add_chunks(base, toks, projs):
    n = len(toks)

    def kernel(base_ref, *refs):
        total = base_ref[...]
        for tok, proj in zip(refs[:n], refs[n : 2 * n]):
            total = total + dot_nt(tok[...], proj[...])
        refs[2 * n][...] = total

    return pl.pallas_call(
        kernel,
        out_shape=jax.ShapeDtypeStruct(base.shape, base.dtype),
        in_specs=[VMEM] * (1 + 2 * n),
        out_specs=VMEM,
        compiler_params=SMALL,
        cost_estimate=cost(),
    )(base, *toks, *projs)


def partial_scores(q_halves, f_stack):
    q_high, q_low = q_halves
    both = dot_nt(f_stack, q_high)
    return both[:TRAJ_DEV] + both[TRAJ_DEV:] + dot_nt(f_stack, q_low)[:TRAJ_DEV]


def spread_blocks(scores, places, slots):
    rows = scores.shape[1] // len(places)
    block = lax.broadcasted_iota(jnp.int32, (TRAJ_DEV, rows * slots), 1) // rows
    ordered = jnp.zeros((TRAJ_DEV, rows * slots), jnp.float32)
    for s, place in enumerate(places):
        piece = scores[:, s * rows : (s + 1) * rows]
        ordered = jnp.where(block == place, jnp.concatenate([piece] * slots, axis=1), ordered)
    return ordered


def gradients(
    table, in_side, out_side, bases, segments, loss_mask, numbered, pieces, slots
):
    count, rank = bases[0].shape
    rows, flat_width = pieces[0].shape
    acts, in_projs = in_side
    grads, out_projs = out_side
    n, m, k = len(in_projs), len(out_projs), len(pieces)

    def kernel(*refs):
        table_ref = table()
        tok_refs, refs = refs[: n + m], refs[n + m :]
        proj_refs, piece_refs, refs = refs[: n + m], refs[n + m : n + m + k], refs[n + m + k :]
        parts = [dot_nt(tok[...], proj[...]) for tok, proj in zip(tok_refs, proj_refs)]
        in_base, out_base, seg_ref, mask_ref, stack_ref, score_ref = refs
        q_halves = halves(jnp.concatenate([ref[...] for ref in piece_refs], axis=0))
        own = seg_ref[...] == lax.broadcasted_iota(jnp.int32, (TRAJ_DEV, count), 0)
        masked = jnp.where(own, mask_ref[...].astype(jnp.float32), 0.0)
        counts = jnp.sum(masked, axis=1, keepdims=True)
        weight = masked * (1.0 / jnp.maximum(counts, 1.0))
        in_t = sum(parts[:n], in_base[...]).T
        t_high, t_low = halves(jnp.concatenate([in_t, in_t], axis=0))
        out_t = sum(parts[n:], out_base[...]).T
        left = (out_t[:, None, :] * weight[None]).reshape(rank * TRAJ_DEV, count)
        l_high, l_low = halves(left)
        outer = dot_nt(
            jnp.concatenate([l_high, l_low], axis=1), jnp.concatenate([t_high, t_high], axis=1)
        ) + dot_nt(l_high, t_low)
        outer = outer.reshape(rank // 2, 2, TRAJ_DEV, 2 * rank)
        low = lax.broadcasted_iota(jnp.int32, (TRAJ_DEV, 2 * rank), 1) < rank
        flat = jnp.concatenate(
            [jnp.where(low, outer[p, 0], outer[p, 1]) for p in range(rank // 2)], axis=1
        )
        f_stack = jnp.concatenate(halves(flat), axis=0)
        scores = partial_scores(q_halves, f_stack)
        stack_ref[...] = f_stack
        score_ref[...] = spread_blocks(scores, [table_ref[p] for p in numbered], slots)

    return pl.pallas_call(
        kernel,
        out_shape=(
            jax.ShapeDtypeStruct((2 * TRAJ_DEV, flat_width), jnp.bfloat16),
            jax.ShapeDtypeStruct((TRAJ_DEV, rows * slots), jnp.float32),
        ),
        in_specs=[VMEM] * (2 * (n + m) + k + 4),
        out_specs=(VMEM, VMEM),
        compiler_params=SMALL,
        cost_estimate=cost(),
    )(
        *acts,
        *grads,
        *in_projs,
        *out_projs,
        *pieces,
        *bases,
        segments,
        loss_mask,
    )


def last_block(table, numbered, scores, f_stack, here, there):
    slots = scores.shape[1] // here.shape[0]

    def kernel(base_ref, stack_ref, here_ref, there_ref, score_ref):
        table_ref = table()
        block = jnp.where(table_ref[numbered[1]] == 0, here_ref[...], there_ref[...])
        scores = partial_scores(halves(block), stack_ref[...])
        score_ref[...] = base_ref[...] + spread_blocks(scores, [table_ref[numbered[0]]], slots)

    return pl.pallas_call(
        kernel,
        out_shape=jax.ShapeDtypeStruct(scores.shape, jnp.float32),
        in_specs=[VMEM] * 4,
        out_specs=VMEM,
        compiler_params=SMALL,
        cost_estimate=cost(),
    )(scores, f_stack, here, there)


def cost():
    return pl.CostEstimate(flops=1, bytes_accessed=1, transcendentals=0)


def fetch_queries(queries, sizes):
    n = sizes["traj"]
    if n != 4:
        return [lax.all_gather(queries, "traj", axis=0, tiled=True)]
    line = range(n)
    beside = lax.ppermute(
        queries,
        ("traj", "sub"),
        [(2 * ((z + 1) % n), 2 * z) for z in line]
        + [(2 * ((z + n - 1) % n) + 1, 2 * z + 1) for z in line],
    )
    across = lax.ppermute(queries, ("traj", "sub"), [(2 * ((z + 2) % n), 2 * z) for z in line])
    return [beside, across]


def body(sizes, activations, out_grads, segments, loss_mask, proj_in, proj_out, queries):
    chips, width = sizes["fsdp"], proj_in.shape[1]

    def to_core(a):
        return lax.ppermute(a, "sub", [(0, 1), (1, 0)])

    def from_chip(a, d):
        return lax.ppermute(a, "fsdp", [((i + d) % chips, i) for i in range(chips)])

    def after(arrays, *waited):
        return lax.optimization_barrier((arrays, *waited))

    far_in = [from_chip(proj_in, d) for d in range(1, chips)]
    far_out = [from_chip(proj_out, d) for d in range(1, chips)]
    fetched = fetch_queries(queries, sizes)
    on_line = len(fetched) > 1

    far_own, far_other = [2 * d for d in range(1, chips)], [2 * d + 1 for d in range(1, chips)]
    numbered = [2 * chips + s for s in range(5)]

    def table():
        x, core = lax.axis_index("fsdp"), lax.axis_index("sub")
        chunks = [2 * lax.rem(x + d, chips) + c for d in range(chips) for c in (core, 1 - core)]
        if not on_line:
            return chunks + [0]
        at, step = lax.axis_index("traj"), 1 + 2 * core
        blocks = [at, at + step, at + 4 - step, at + 2]
        return chunks + [lax.rem(b, 4) for b in blocks] + [core]

    in_sum, out_sum = project(
        [(activations, [proj_in], [0]), (out_grads, [proj_out], [0])],
        table,
        [],
    )
    first = fetched[:1] if on_line else []
    far_in, first, late_out, in_sum, out_sum = after(far_in, first, proj_out, in_sum, out_sum)
    fetched = first + fetched[len(first) :]
    others_in = [to_core(a) for a in far_in]
    other_out = to_core(late_out)
    (in_sum,) = project([(activations, far_in, far_own)], table, [in_sum])
    in_sum, other_in = after(in_sum, to_core(proj_in))
    others_in = others_in + [other_in]
    if on_line:
        beside, across = fetched
        beside_other = to_core(beside)
    else:
        pieces = fetched
    chunk = table()
    activations, out_grads, in_sum = after(activations, out_grads, in_sum)
    cut = [
        [
            lax.dynamic_slice_in_dim(array, chunk[place] * width, width, 1)
            for place in places
        ]
        for array, places in (
            (out_grads, far_own),
            (activations, far_other + [1]),
            (out_grads, far_other + [1]),
        )
    ]
    far_out, in_sum, cut = after(far_out, in_sum, cut)
    grads_own, acts_other, grads_other = cut
    if on_line:
        far_out, beside = after(far_out, beside)
        pieces = [queries, beside, beside_other]
    others_out = [to_core(a) for a in far_out] + [other_out]
    out_sum = add_chunks(out_sum, grads_own, far_out)
    if on_line:
        across, out_sum = after(across, out_sum)
        across_other = to_core(across)
    f_stack, scores = gradients(
        table,
        (acts_other, others_in),
        (grads_other, others_out),
        (in_sum, out_sum),
        segments,
        loss_mask,
        numbered[: len(pieces)],
        pieces,
        4 if on_line else 1,
    )
    if on_line:
        scores = last_block(table, numbered[3:], scores, f_stack, across, across_other)
    return scores.T


def solution(mesh):
    placed = (
        P(("groups", "traj", "fsdp", "sub"), None),
        P(("groups", "traj", "fsdp", "sub"), None),
        P(("groups", "traj", "fsdp", "sub"), None),
        P(("groups", "traj", "fsdp", "sub"), None),
        P(None, ("fsdp", "sub")),
        P(None, ("fsdp", "sub")),
        P(("groups", "traj"), None),
    )
    sizes = dict(mesh.shape)

    def program(*arrays):
        return body(sizes, *arrays)

    return jax.shard_map(
        program,
        mesh=mesh,
        in_specs=placed,
        out_specs=P("groups", ("traj", "fsdp", "sub")),
        check_vma=False,
    )
```
